256 devices in a mesh: blk: 32 (over z, x_lo, core), group: 8 (over y, x_hi).
Axes of the slice: x: 4 (x_hi: 2, x_lo: 2; x = x_hi * 2 + x_lo), y: 4, z: 8, core: 2. Of those that a mesh axis runs over, the one named last changes fastest.
Arguments:
- image: float32 [16384, 1024], P('blk'), may hold values from -8 to 8
- text: float32 [16384, 1024], P(('blk', 'group')), may hold values from -8 to 8
Outputs:
- grad_image: float32 [16384, 1024], P('blk')
- grad_text: float32 [16384, 1024], P(('blk', 'group'))
The draws below stay inside these ranges and needn't reach their ends.
All inputs are finite; a program needn't handle non-finite values.
Results may differ from the reference program's by a relative error of at most 0.0003.
Values sent between devices are 32-bit elements; how exact they have to be, the bound alone decides.
No kernel may reach another device: no remote copies, remote signals or barrier semaphores. Data moves between devices by JAX's collectives and lax.ppermute only.
A program may use at most 64 MiB of HBM per device.

```python
import math
import jax
import jax.numpy as jnp
from jax import lax

D = 1024
BATCH = 16384


def paired(key):
    keys = jax.random.split(key, 9)

    def base(first, second):
        normal_part = jax.random.normal(first, (BATCH, D), jnp.float32)
        return normal_part
    image = 0.25 * base(keys[0], keys[1])
    text = 0.25 * base(keys[2], keys[3])
    level = math.sqrt(100.0 / D)
    signs = jax.random.normal(keys[8], (BATCH, D), jnp.float32)
    planted_vec = jnp.where(signs >= 0.0, level, -level)
    positions = jnp.arange(BATCH, dtype=jnp.int32)
    phase = positions % 256
    leading = jnp.take(planted_vec, positions - phase, axis=0)
    strength = (2.0 + (positions // 256 % 3).astype(jnp.float32))[:, None]
    image_noise = jax.random.normal(keys[6], (BATCH, D), jnp.float32)
    text_noise = jax.random.normal(keys[7], (BATCH, D), jnp.float32)
    first_row = (phase == 0)[:, None]
    second_row = (phase == 1)[:, None]
    image = jnp.where(first_row, leading, image)
    image = jnp.where(second_row, 0.99 * leading + 0.01 * image_noise, image)
    text = jnp.where(first_row, strength * leading, text)
    text = jnp.where(second_row, 0.99 * strength * leading + 0.05 * text_noise, text)
    return (jnp.clip(image, -8.0, 8.0), jnp.clip(text, -8.0, 8.0))


def draw_image(key, part):
    return paired(key)[0]


def draw_text(key, part):
    return paired(key)[1]


def setup_inputs(seed: int = 0) -> dict:
    streams_of = jax.random.split(jax.random.key(seed), 3)
    return {
        "image": draw_image(jax.random.fold_in(streams_of[2], 71), 0),
        "text": draw_text(jax.random.fold_in(streams_of[2], 71), 0),
    }


PRECISE = lax.Precision.HIGHEST


def reference(image, text):
    span = math.gcd(BATCH, 512)
    number = BATCH // span
    blocks = image.reshape(number, span, D)

    def gather_stats(carry, block):
        column_peak, column_total = carry
        scores = jnp.dot(block, text.T, precision=PRECISE, preferred_element_type=jnp.float32)
        row_peak = jnp.max(scores, axis=1)
        row_level = row_peak + jnp.log(jnp.sum(jnp.exp(scores - row_peak[:, None]), axis=1))
        new_peak = jnp.maximum(column_peak, jnp.max(scores, axis=0))
        column_total = column_total * jnp.exp(column_peak - new_peak) + jnp.sum(jnp.exp(scores - new_peak[None, :]), axis=0)
        return (new_peak, column_total), row_level

    start_carry = (jnp.full((BATCH,), -jnp.inf, jnp.float32), jnp.zeros((BATCH,), jnp.float32))
    (column_peak, column_total), row_levels = lax.scan(gather_stats, start_carry, blocks)
    column_level = column_peak + jnp.log(column_total)
    columns = jnp.arange(BATCH, dtype=jnp.int32)

    def gradients(grad_text, inputs):
        block, row_level, index = inputs
        scores = jnp.dot(block, text.T, precision=PRECISE, preferred_element_type=jnp.float32)
        rows = index * span + jnp.arange(span, dtype=jnp.int32)
        same_pair = (rows[:, None] == columns[None, :]).astype(jnp.float32)
        weights = 0.5 * jnp.exp(scores - row_level[:, None]) + 0.5 * jnp.exp(scores - column_level[None, :]) - same_pair
        grad_block = jnp.dot(weights, text, precision=PRECISE, preferred_element_type=jnp.float32)
        grad_text = grad_text + jnp.dot(weights.T, block, precision=PRECISE, preferred_element_type=jnp.float32)
        return grad_text, grad_block

    inputs = (blocks, row_levels, jnp.arange(number, dtype=jnp.int32))
    grad_text, grad_blocks = lax.scan(gradients, jnp.zeros((BATCH, D), jnp.float32), inputs)
    return grad_blocks.reshape(BATCH, D), grad_text
```

```python
import jax
import jax.numpy as jnp
from jax import lax
from jax.sharding import Mesh, PartitionSpec as P

FULL = lax.Precision.HIGHEST
THREE = lax.Precision.HIGH
ORDER = (0, 1, 7, 2, 6, 3, 5, 4)
PLACE = tuple(ORDER.index(k) for k in range(8))


def x_other():
    pairs = []
    for x in range(4):
        t = (x - 1) % 4 if x % 2 == 0 else (x + 1) % 4
        pairs.append(((x % 2) * 2 + x // 2, (t % 2) * 2 + t // 2))
    return pairs


def join_levels(levels):
    top = jnp.max(levels, axis=0)
    return top + jnp.log(jnp.sum(jnp.exp(levels - top[None]), axis=0))


def swap_core(a):
    return lax.ppermute(a, "core", [(0, 1), (1, 0)])


def swap_x(near, far):
    return (
        lax.ppermute(near, "xl", [(0, 1), (1, 0)]),
        lax.ppermute(far, ("xl", "xh"), x_other()),
    )


def local(image, text):
    rows, width = image.shape
    part = text.shape[0]
    z, xl, core = (lax.axis_index(a) for a in ("z", "xl", "core"))
    group = lax.axis_index("y") * 2 + lax.axis_index("xh")
    half = rows // 2

    chunks = {0: text}
    for k in (1, 7, 2, 6, 3, 5, 4):
        chunks[k] = lax.ppermute(text, "z", [(i, (i + k) % 8) for i in range(8)])
    near, far = swap_x(image[:half], image[half:])
    both = jnp.concatenate([image, near, far], axis=0)

    texts, scores = [], []
    for b in range(2):
        mine = jnp.concatenate([chunks[k] for k in ORDER[4 * b : 4 * b + 4]], axis=0)
        texts.append(jnp.concatenate([mine, swap_core(mine)], axis=0))
        scores.append(
            jnp.einsum("id,td->it", both, texts[b], precision=FULL, preferred_element_type=jnp.float32)
        )
    scores = jnp.concatenate(scores, axis=1)
    piece = jnp.concatenate(texts, axis=0)

    row_top = jnp.max(scores, axis=1)
    row_part = row_top + jnp.log(jnp.sum(jnp.exp(scores - row_top[:, None]), axis=1))
    col_top = jnp.max(scores, axis=0)
    col_part = col_top + jnp.log(jnp.sum(jnp.exp(scores - col_top[None, :]), axis=0))

    r = row_part.reshape(2, rows)
    r = jnp.where(xl == 0, r, r[::-1])
    r = jnp.broadcast_to(r.reshape(1, -1), (16, 2 * rows))
    r = join_levels(lax.all_to_all(r, ("xl", "y", "xh"), 0, 0, tiled=True)).reshape(2, rows)
    row_level = jnp.where(xl == 0, r, r[::-1]).reshape(-1)

    c = col_part.reshape(2, 2, 4, part).transpose(1, 0, 2, 3).reshape(2, 8, part)
    c = jnp.where(core == 0, c, c[::-1])[:, jnp.array(PLACE), :]
    turn = (z - jnp.arange(8)) % 8
    c = jnp.take(c, turn, axis=1)
    c = jnp.broadcast_to(c.reshape(1, -1), (16, 16 * part))
    c = join_levels(lax.all_to_all(c, ("z", "core"), 0, 0, tiled=True)).reshape(2, 8, part)
    c = jnp.take(c, turn, axis=1)[:, jnp.array(ORDER), :]
    c = jnp.where(core == 0, c, c[::-1])
    col_level = c.reshape(2, 2, 4, part).transpose(1, 0, 2, 3).reshape(-1)

    i = jnp.arange(2 * rows)[:, None]
    j = jnp.arange(16 * part)[None, :]
    same = (j < part) & (i == group * part + j)
    weights = (
        0.5 * jnp.exp(scores - row_level[:, None])
        + 0.5 * jnp.exp(scores - col_level[None, :])
        - same.astype(jnp.float32)
    )

    def times_text(w):
        return jnp.einsum("it,td->id", w, piece, precision=THREE, preferred_element_type=jnp.float32)

    away = times_text(weights[rows:])
    got = swap_x(away[:half], away[half:])
    g_text = jnp.einsum("it,id->td", weights, both, precision=THREE, preferred_element_type=jnp.float32)
    home = times_text(weights[:rows])

    g_text = g_text.reshape(2, 2, 4 * part, width)
    g_text = g_text[:, 0] + swap_core(g_text[:, 1])
    g_text = g_text.reshape(8, part, width)
    g_text = jnp.concatenate(
        [
            lax.dynamic_index_in_dim(g_text, jnp.array(PLACE)[(z - zz) % 8], 0)
            for zz in range(8)
        ],
        axis=0,
    ).reshape(8 * part, width)
    grad_text = lax.psum_scatter(g_text, "z", scatter_dimension=0, tiled=True)

    home = home + jnp.concatenate(got, axis=0)
    home = lax.all_to_all(home.reshape(8, part, width), ("y", "xh"), 0, 0, tiled=True)
    mine = jnp.sum(home.reshape(8, part, width), axis=0)
    out = jnp.broadcast_to(mine[None], (8, part, width))
    out = lax.all_to_all(out, ("y", "xh"), 0, 0, tiled=True)
    return out.reshape(rows, width), grad_text


def solution(mesh):
    fine = Mesh(mesh.devices.reshape(8, 2, 2, 4, 2), ("z", "xl", "core", "y", "xh"))
    blk = ("z", "xl", "core")
    placed = (P(blk, None), P(blk + ("y", "xh"), None))
    return jax.shard_map(local, mesh=fine, in_specs=placed, out_specs=placed, check_vma=False)
```

```python
import functools

import jax
import jax.numpy as jnp
from jax import lax
from jax.experimental import pallas as pl
from jax.experimental.pallas import tpu as pltpu
from jax.sharding import Mesh, PartitionSpec as P

Z, Y = 8, 4
STEP = 256
CUTS = 8
PARTS = 2
PICK = 100_000_000
F32, BF16 = jnp.float32, jnp.bfloat16
VMEM = pl.BlockSpec(memory_space=pltpu.VMEM)
SMEM = pl.BlockSpec(memory_space=pltpu.SMEM)


def call(kernel, name, outs, n_in, scalars=False, scratch=(), cost=1000):
    in_specs = [VMEM] * n_in
    if scalars:
        in_specs = [SMEM] + in_specs
    return pl.pallas_call(
        kernel,
        out_shape=tuple(jax.ShapeDtypeStruct(s, t) for s, t in outs),
        in_specs=in_specs,
        out_specs=(VMEM,) * len(outs),
        scratch_shapes=scratch,
        compiler_params=pltpu.CompilerParams(vmem_limit_bytes=24 * 1024 * 1024),
        cost_estimate=pl.CostEstimate(flops=1000, bytes_accessed=cost, transcendentals=0),
        name=name,
    )


def grid_call(kernel, name, steps, ins, outs, scratch=(), cost=1000):
    run = pl.pallas_call(
        kernel,
        grid=(steps,),
        out_shape=tuple(pltpu.HBM(s, t) for s, t, _ in outs),
        in_specs=list(ins),
        out_specs=tuple(spec for _, _, spec in outs),
        scratch_shapes=scratch,
        compiler_params=pltpu.CompilerParams(
            vmem_limit_bytes=40 * 1024 * 1024, dimension_semantics=("arbitrary",)
        ),
        cost_estimate=pl.CostEstimate(flops=1000, bytes_accessed=cost, transcendentals=0),
        name=name,
    )

    def apply(*args):
        return run(
            *[
                a if spec is SMEM else pltpu.with_memory_space_constraint(a, pltpu.HBM)
                for a, spec in zip(args, ins)
            ]
        )

    return apply


def rows_at(block, start=0):
    return pl.BlockSpec(block, lambda i: (i + start, 0))


def whole(block):
    return pl.BlockSpec(block, lambda i: (0,) * len(block))


def ring(n, step):
    return [(i, (i + step) % n) for i in range(n)]


def flip(a, axis, size, bit):
    return lax.ppermute(a, axis, [(i, i ^ bit) for i in range(size)])


def x_other():
    pairs = []
    for x in range(4):
        t = (x - 1) % 4 if x % 2 == 0 else (x + 1) % 4
        pairs.append(((x % 2) * 2 + x // 2, (t % 2) * 2 + t // 2))
    return pairs


def swap_x(near, far):
    return flip(near, "xl", 2, 1), lax.ppermute(far, ("xl", "xh"), x_other())


def join(a, b):
    top = jnp.maximum(a, b)
    return top + jnp.log(1.0 + jnp.exp(jnp.minimum(a, b) - top))


def split2(a):
    high = a.astype(BF16)
    return high, (a - high.astype(F32)).astype(BF16)


def split3(a):
    high = a.astype(BF16)
    rest = a - high.astype(F32)
    mid = rest.astype(BF16)
    return high, mid, (rest - mid.astype(F32)).astype(BF16)


def dot(a, b, dims=((1,), (0,))):
    return lax.dot_general(a, b, (dims, ((), ())), preferred_element_type=F32)


def scores_kernel(first, place, *refs):
    i = pl.program_id(0)
    if first:
        image_ref, near_ref, far_ref, text_ref = refs[:4]
        s_ref, th_ref, tm_ref, r_ref, c_ref, ih_ref, im_ref, il_ref = refs[4:12]
    else:
        ih_ref, im_ref, il_ref, r_in, c_in, text_ref = refs[:6]
        s_ref, th_ref, tm_ref, r_ref, c_ref = refs[6:11]
    h_t, m_t, l_t, top, total = refs[-5:]

    @pl.when(i == 0)
    def _():
        text = text_ref[...]
        th_ref[...], tm_ref[...] = split2(text)
        h_t[...], m_t[...], l_t[...] = split3(text.T)
        top[...] = jnp.full(top.shape, -jnp.inf, F32)
        total[...] = jnp.zeros(total.shape, F32)
        if first:
            c_ref[...] = jnp.zeros(c_ref.shape, F32)
        else:
            c_ref[...] = c_in[...]

    if first:
        a = jnp.where(i < 2, image_ref[...], jnp.where(i == 2, near_ref[...], far_ref[...]))
        ih_ref[...], im_ref[...], il_ref[...] = split3(a)
    ih, im, il = ih_ref[...], im_ref[...], il_ref[...]
    th, tm, tl = h_t[...], m_t[...], l_t[...]
    small = dot(ih, tl) + dot(il, th) + dot(im, tm)
    s = dot(ih, th) + (dot(ih, tm) + dot(im, th) + small)
    s_ref[...] = s
    high = jnp.max(s, axis=1, keepdims=True)
    row = high + jnp.log(jnp.sum(jnp.exp(s - high), axis=1, keepdims=True))
    row = jnp.broadcast_to(row, (row.shape[0], 128)).T[:1, :]
    slot = pl.ds((i + 2 * place[0]) % 4, 1)
    r_ref[slot, :] = row if first else join(row, r_in[slot, :])
    high = jnp.maximum(jnp.max(s, axis=0, keepdims=True), top[...])
    total[...] = total[...] * jnp.exp(top[...] - high) + jnp.sum(jnp.exp(s - high), axis=0, keepdims=True)
    top[...] = high

    @pl.when(i == pl.num_programs(0) - 1)
    def _():
        core = place[1] if first else 1 - place[1]
        c_ref[pl.ds(core, 1), :] = top[...] + jnp.log(total[...])


def weights(s, row, col):
    return 0.5 * jnp.exp(s - row) + 0.5 * jnp.exp(s - col)


def rows_kernel(away, place, s1, s2, r_ref, c_ref, th1, tm1, th2, tm2, *refs):
    i = pl.program_id(0)
    if away:
        near, far = refs[:2]
    kept = refs[2 if away else 1 :]
    part = c_ref.shape[1] // Z

    c1, c2 = (c_ref[pl.ds(a, 1), :] for a in (place[1], 1 - place[1]))
    row = r_ref[pl.ds((i + 2 * away + 2 * place[0]) % 4, 1), :]
    row = jnp.broadcast_to(row, (128, row.shape[1])).T[:, :1]
    total = None
    for b, (s, c, th, tm) in enumerate(((s1, c1, th1, tm1), (s2, c2, th2, tm2))):
        w = weights(s[...], row, c)
        if b == 0 and not away:
            x = lax.broadcasted_iota(jnp.int32, w.shape, 0) + (i * w.shape[0] - place[3])
            y = lax.broadcasted_iota(jnp.int32, w.shape, 1) - place[2] * part
            w = jnp.where((x == y) & (y >= 0) & (y < part), w - 1.0, w)
        wh, wl = split2(w)
        kept[2 * b][...], kept[2 * b + 1][...] = wh, wl
        term = dot(wh, th[...]) + (dot(wh, tm[...]) + dot(wl, th[...]))
        total = term if total is None else total + term
    if not away:
        refs[0][...] = total
    else:

        @pl.when(i == 0)
        def _():
            near[...] = total

        @pl.when(i == 1)
        def _():
            far[...] = total


def text_kernel(home_h, home_l, away_h, away_l, ih, im, *outs):
    tn = ((0,), (0,))
    rows = home_h.shape[0]
    total = None
    for h, l, k in ((home_h, home_l, 0), (away_h, away_l, rows)):
        high, mid = ih[k : k + rows, :], im[k : k + rows, :]
        wh, wl = h[...], l[...]
        term = dot(wh, high, tn) + (dot(wh, mid, tn) + dot(wl, high, tn))
        total = term if total is None else total + term
    if len(outs) == 1:
        outs[0][...] = total
        return
    n = outs[0].shape[0]
    each = total.shape[0] // n
    for k, out in enumerate(outs):

        @pl.when(pl.program_id(0) == k // each)
        def _():
            out[...] = total[k % each * n : (k % each + 1) * n]


def collect_kernel(own, *refs):
    got, out = refs[:-1], refs[-1]
    n = out.shape[0] // len(got)
    for k, ref in enumerate(got):
        at = slice(k * n, (k + 1) * n)
        out[at, :] = own[at, :] + ref[...]


def pick_kernel(place, home_ref, near_ref, far_ref, *outs):
    size, each = outs[0].shape
    for k in range(Y):
        at = (place[4] + k) % Y
        got = pl.ds((at % 2) * size, size)
        total = home_ref[pl.ds(at * size, size), :] + jnp.where(at < 2, near_ref[got, :], far_ref[got, :])
        for p in range(PARTS):
            outs[p * Y + k][...] = total[:, p * each : (p + 1) * each]


def assemble_kernel(place, *refs):
    pieces, out = refs[:-1], refs[-1]
    size, each = pieces[0].shape
    for p in range(PARTS):
        for k in range(Y):
            at = (place[4] + Y - k) % Y
            out[pl.ds(at * size, size), p * each : (p + 1) * each] = pieces[p * Y + k][...]


def local(image, text):
    rows, width = image.shape
    part = text.shape[0]
    z, xl, core, y = (lax.axis_index(a) for a in ("z", "xl", "core", "y"))
    group = y * 2 + lax.axis_index("xh")
    half = rows // 2
    place = jnp.stack([xl, core, z, group * part, y]).astype(jnp.int32)
    tall, steps = (STEP, width), rows // STEP
    table = [((2 * steps, STEP), F32, whole((2 * steps, STEP))), ((2, Z * part), F32, whole((2, Z * part)))]

    near, far = swap_x(image[:half], image[half:])
    line = lax.all_gather(text, "z", axis=0, tiled=True)
    line, near, far = lax.optimization_barrier((line, near, far))
    columns = Z * part
    full = (columns, width)

    s, th, tm = [], [], []
    for b, texts in enumerate((line, flip(line, "core", 2, 1))):
        outs = [
            ((2 * rows, columns), F32, rows_at((STEP, columns))),
            (full, BF16, whole(full)),
            (full, BF16, whole(full)),
        ] + table
        if b == 0:
            ins = [pl.BlockSpec(tall, lambda i: (jnp.minimum(i, 1), 0)), whole(tall), whole(tall)]
            outs += [((2 * rows, width), BF16, rows_at(tall))] * 3
            args = (image, near, far)
        else:
            ins = [rows_at(tall)] * 3 + [spec for _, _, spec in table]
            args = (ih, im, il, r, c)
        out = grid_call(
            functools.partial(scores_kernel, b == 0),
            "scores",
            2 * steps,
            [SMEM] + ins + [whole(full)],
            outs,
            scratch=[pltpu.VMEM((width, columns), BF16)] * 3 + [pltpu.VMEM((1, columns), F32)] * 2,
        )(place, *args, texts)
        s.append(out[0])
        th.append(out[1])
        tm.append(out[2])
        r, c = out[3:5]
        if b == 0:
            ih, im, il = out[5:]

    c = c.reshape(2, Z, part)
    rounds = zip(
        (("y", 4, 1), ("y", 4, 2), ("xl", 2, 1), ("xh", 2, 1)),
        (("core", 2, 1), ("z", 8, 1), ("z", 8, 2), ("z", 8, 4)),
    )
    for row_round, col_round in rounds:
        r, c = join(r, flip(r, *row_round)), join(c, flip(c, *col_round))

    c = c.reshape(2, columns)
    args = (s[0], s[1], r, c, th[0], tm[0], th[1], tm[1])
    sizes = [a.shape[1] for a in s]
    kept = [((rows, n), BF16, rows_at((STEP, n))) for n in sizes for _ in range(2)]
    fixed = [spec for _, _, spec in table] + [whole((n, width)) for n in sizes for _ in range(2)]
    away = grid_call(
        functools.partial(rows_kernel, 1),
        "away",
        steps,
        [SMEM] + [rows_at((STEP, n), steps) for n in sizes] + fixed,
        [((half, width), F32, whole((half, width)))] * 2 + kept,
    )(place, *args)
    got = swap_x(*away[:2])
    kept_away = away[2:]
    late, _ = lax.optimization_barrier((args, away[0]))
    home = grid_call(
        functools.partial(rows_kernel, 0),
        "home",
        steps,
        [SMEM] + [rows_at((STEP, n)) for n in sizes] + fixed,
        [((rows, width), F32, rows_at(tall))] + kept,
    )(place, *late)
    home, kept_home = home[0], home[1:]

    def make_text(b, name, outs):
        wide = pl.BlockSpec((rows, STEP), lambda i: (0, i))
        return grid_call(
            text_kernel,
            name,
            columns // STEP,
            [wide] * 4 + [whole((2 * rows, width))] * 2,
            outs,
        )(*kept_home[2 * b : 2 * b + 2], *kept_away[2 * b : 2 * b + 2], ih, im)

    piece = (columns // CUTS, width)
    other = make_text(1, "text_other", [(piece, F32, whole(piece))] * CUTS)
    (own,) = make_text(0, "text_own", [(full, F32, rows_at(tall))])
    pieces = [flip(a, "core", 2, 1) for a in other]
    (g_text,) = call(collect_kernel, "collect", [(full, F32)], 1 + len(pieces))(own, *pieces)
    g_text, *got = lax.optimization_barrier((g_text, *got))
    grad_text = lax.psum_scatter(g_text, "z", scatter_dimension=0, tiled=True)

    quarter = rows // Y
    mine = call(
        pick_kernel, "pick", [((quarter, width // PARTS), F32)] * (PARTS * Y), 3, scalars=True, cost=PICK
    )(place, home, *got)
    pieces = []
    for p in range(PARTS):
        own = mine[p * Y] + sum(lax.ppermute(mine[p * Y + k], "y", ring(Y, k)) for k in (1, 3, 2))
        own = own + flip(own, "xh", 2, 1)
        pieces += [own] + [lax.ppermute(own, "y", ring(Y, k)) for k in (1, 2, 3)]
    (out,) = call(assemble_kernel, "assemble", [((rows, width), F32)], PARTS * Y, scalars=True)(place, *pieces)
    return out, grad_text


def solution(mesh):
    fine = Mesh(mesh.devices.reshape(Z, 2, 2, Y, 2), ("z", "xl", "core", "y", "xh"))
    blk = ("z", "xl", "core")
    placed = (P(blk, None), P(blk + ("y", "xh"), None))
    return jax.shard_map(local, mesh=fine, in_specs=placed, out_specs=placed, check_vma=False)
```

```python
import functools

import jax
import jax.numpy as jnp
from jax import lax
from jax.experimental import pallas as pl
from jax.experimental.pallas import tpu as pltpu
from jax.sharding import Mesh, PartitionSpec as P

Z, Y = 8, 4
STEP = 256
CUTS = 8
WIDE = 512
PICK = 100_000_000
F32, BF16 = jnp.float32, jnp.bfloat16
VMEM = pl.BlockSpec(memory_space=pltpu.VMEM)
SMEM = pl.BlockSpec(memory_space=pltpu.SMEM)


def call(kernel, name, outs, n_in, scalars=False, scratch=(), cost=1000):
    in_specs = [VMEM] * n_in
    if scalars:
        in_specs = [SMEM] + in_specs
    return pl.pallas_call(
        kernel,
        out_shape=tuple(jax.ShapeDtypeStruct(s, t) for s, t in outs),
        in_specs=in_specs,
        out_specs=(VMEM,) * len(outs),
        scratch_shapes=scratch,
        compiler_params=pltpu.CompilerParams(vmem_limit_bytes=24 * 1024 * 1024),
        cost_estimate=pl.CostEstimate(flops=1000, bytes_accessed=cost, transcendentals=0),
        name=name,
    )


def grid_call(kernel, name, steps, ins, outs, scratch=(), cost=1000, free_in=(), free_out=()):
    run = pl.pallas_call(
        kernel,
        grid=(steps,),
        out_shape=tuple(
            jax.ShapeDtypeStruct(s, t) if k in free_out else pltpu.HBM(s, t) for k, (s, t, _) in enumerate(outs)
        ),
        in_specs=list(ins),
        out_specs=tuple(spec for _, _, spec in outs),
        scratch_shapes=scratch,
        compiler_params=pltpu.CompilerParams(
            vmem_limit_bytes=40 * 1024 * 1024, dimension_semantics=("arbitrary",)
        ),
        cost_estimate=pl.CostEstimate(flops=1000, bytes_accessed=cost, transcendentals=0),
        name=name,
    )

    def apply(*args):
        return run(
            *[
                a if k == 0 and ins[0] is SMEM or k in free_in else pltpu.with_memory_space_constraint(a, pltpu.HBM)
                for k, a in enumerate(args)
            ]
        )

    return apply


def rows_at(block, start=0):
    return pl.BlockSpec(block, lambda i: (i + start, 0))


def whole(block):
    return pl.BlockSpec(block, lambda i: (0,) * len(block))


def ring(n, step):
    return [(i, (i + step) % n) for i in range(n)]


def flip(a, axis, size, bit):
    return lax.ppermute(a, axis, [(i, i ^ bit) for i in range(size)])


def x_other():
    pairs = []
    for x in range(4):
        t = (x - 1) % 4 if x % 2 == 0 else (x + 1) % 4
        pairs.append(((x % 2) * 2 + x // 2, (t % 2) * 2 + t // 2))
    return pairs


def swap_x(near, far):
    return flip(near, "xl", 2, 1), lax.ppermute(far, ("xl", "xh"), x_other())


def join(a, b):
    top = jnp.maximum(a, b)
    return top + jnp.log(1.0 + jnp.exp(jnp.minimum(a, b) - top))


def split2(a):
    high = a.astype(BF16)
    return high, (a - high.astype(F32)).astype(BF16)


def split3(a):
    high = a.astype(BF16)
    rest = a - high.astype(F32)
    mid = rest.astype(BF16)
    return high, mid, (rest - mid.astype(F32)).astype(BF16)


def dot(a, b, dims=((1,), (0,))):
    return lax.dot_general(a, b, (dims, ((), ())), preferred_element_type=F32)


def scores_kernel(first, place, *refs):
    i = pl.program_id(0)
    if first:
        image_ref, near_ref, far_ref, text_ref = refs[:4]
        s_ref, th_ref, tm_ref, r_ref, c_ref, ih_ref, im_ref, il_ref = refs[4:12]
    else:
        ih_ref, im_ref, il_ref, r_in, c_in, text_ref = refs[:6]
        s_ref, th_ref, tm_ref, r_ref, c_ref = refs[6:11]
    h_t, m_t, l_t, top, total = refs[-5:]

    @pl.when(i == 0)
    def _():
        text = text_ref[...]
        th_ref[...], tm_ref[...] = split2(text)
        h_t[...], m_t[...], l_t[...] = split3(text.T)
        top[...] = jnp.full(top.shape, -jnp.inf, F32)
        total[...] = jnp.zeros(total.shape, F32)
        if first:
            c_ref[...] = jnp.zeros(c_ref.shape, F32)
        else:
            c_ref[...] = c_in[...]

    if first:
        a = jnp.where(i < 2, image_ref[...], jnp.where(i == 2, near_ref[...], far_ref[...]))
        ih_ref[...], im_ref[...], il_ref[...] = split3(a)
    ih, im, il = ih_ref[...], im_ref[...], il_ref[...]
    th, tm, tl = h_t[...], m_t[...], l_t[...]
    small = dot(ih, tl) + dot(il, th) + dot(im, tm)
    s = dot(ih, th) + (dot(ih, tm) + dot(im, th) + small)
    s_ref[...] = s
    high = jnp.max(s, axis=1, keepdims=True)
    row = high + jnp.log(jnp.sum(jnp.exp(s - high), axis=1, keepdims=True))
    row = jnp.broadcast_to(row, (row.shape[0], 128)).T[:1, :]
    slot = pl.ds((i + 2 * place[0]) % 4, 1)
    r_ref[slot, :] = row if first else join(row, r_in[slot, :])
    high = jnp.maximum(jnp.max(s, axis=0, keepdims=True), top[...])
    total[...] = total[...] * jnp.exp(top[...] - high) + jnp.sum(jnp.exp(s - high), axis=0, keepdims=True)
    top[...] = high

    @pl.when(i == pl.num_programs(0) - 1)
    def _():
        core = place[1] if first else 1 - place[1]
        c_ref[pl.ds(core, 1), :] = top[...] + jnp.log(total[...])


def weights(s, row, col):
    return 0.5 * jnp.exp(s - row) + 0.5 * jnp.exp(s - col)


def rows_kernel(away, place, s1, s2, r_ref, c_ref, th1, tm1, th2, tm2, *refs):
    i = pl.program_id(0)
    if away:
        near, far = refs[:2]
    kept = refs[2 if away else 1 :]
    part = c_ref.shape[1] // Z

    c1, c2 = (c_ref[pl.ds(a, 1), :] for a in (place[1], 1 - place[1]))
    row = r_ref[pl.ds((i + 2 * away + 2 * place[0]) % 4, 1), :]
    row = jnp.broadcast_to(row, (128, row.shape[1])).T[:, :1]
    total = None
    for b, (s, c, th, tm) in enumerate(((s1, c1, th1, tm1), (s2, c2, th2, tm2))):
        w = weights(s[...], row, c)
        if b == 0 and not away:
            x = lax.broadcasted_iota(jnp.int32, w.shape, 0) + (i * w.shape[0] - place[3])
            y = lax.broadcasted_iota(jnp.int32, w.shape, 1) - place[2] * part
            w = jnp.where((x == y) & (y >= 0) & (y < part), w - 1.0, w)
        wh, wl = split2(w)
        kept[2 * b][...], kept[2 * b + 1][...] = wh, wl
        term = dot(wh, th[...]) + (dot(wh, tm[...]) + dot(wl, th[...]))
        total = term if total is None else total + term
    if not away:
        refs[0][...] = total
    else:

        @pl.when(i == 0)
        def _():
            near[...] = total

        @pl.when(i == 1)
        def _():
            far[...] = total


def text_kernel(home_h, home_l, away_h, away_l, ih, im, *outs):
    tn = ((0,), (0,))
    rows = home_h.shape[0]
    total = None
    for h, l, k in ((home_h, home_l, 0), (away_h, away_l, rows)):
        high, mid = ih[k : k + rows, :], im[k : k + rows, :]
        wh, wl = h[...], l[...]
        term = dot(wh, high, tn) + (dot(wh, mid, tn) + dot(wl, high, tn))
        total = term if total is None else total + term
    if len(outs) == 1:
        outs[0][...] = total
        return
    n = outs[0].shape[0]
    each = total.shape[0] // n
    for k, out in enumerate(outs):

        @pl.when(pl.program_id(0) == k // each)
        def _():
            out[...] = total[k % each * n : (k % each + 1) * n]


def collect_kernel(own, *refs):
    got, out = refs[:-1], refs[-1]
    n = out.shape[0] // len(got)
    for k, ref in enumerate(got):
        at = slice(k * n, (k + 1) * n)
        out[at, :] = own[at, :] + ref[...]


def pick_kernel(place, home_ref, near_ref, far_ref, *outs):
    size, each = outs[0].shape
    for k in range(Y):
        at = (place[4] + k) % Y
        got = pl.ds((at % 2) * size, size)
        outs[k][...] = home_ref[pl.ds(at * size, size), :each] + jnp.where(
            at < 2, near_ref[got, :each], far_ref[got, :each]
        )
    half = near_ref.shape[0]
    for out, at in ((outs[Y], place[5]), (outs[Y + 1], 1 - place[5])):
        out[...] = home_ref[pl.ds(at * half, half), each:] + jnp.where(at == 0, near_ref[:, each:], far_ref[:, each:])


def turn_kernel(place, kept, got, *outs):
    size = outs[0].shape[0]
    for k in range(Y):
        at = pl.ds((place[4] + k) % Y * size, size)
        outs[k][...] = kept[at, :] + got[at, :]


def gather_kernel(place, *refs):
    pieces, out = refs[:-1], refs[-1]
    size = pieces[0].shape[0]
    for k in range(Y):
        out[pl.ds((place[4] + Y - k) % Y * size, size), :] = pieces[k][...]


def assemble_kernel(place, *refs):
    pieces, halves, out = refs[:Y], refs[Y:-1], refs[-1]
    size, each = pieces[0].shape
    for k in range(Y):
        out[pl.ds((place[4] + Y - k) % Y * size, size), :each] = pieces[k][...]
    size = halves[0].shape[0]
    for half, at in ((halves[0], place[5]), (halves[1], 1 - place[5])):
        out[pl.ds(at * size, size), each:] = half[...]


def local(image, text):
    rows, width = image.shape
    part = text.shape[0]
    z, xl, core, y = (lax.axis_index(a) for a in ("z", "xl", "core", "y"))
    group = y * 2 + lax.axis_index("xh")
    half = rows // 2
    place = jnp.stack([xl, core, z, group * part, y, lax.axis_index("xh")]).astype(jnp.int32)
    tall, steps = (STEP, width), rows // STEP
    table = [((2 * steps, STEP), F32, whole((2 * steps, STEP))), ((2, Z * part), F32, whole((2, Z * part)))]

    near, far = swap_x(image[:half], image[half:])
    line = lax.all_gather(text, "z", axis=0, tiled=True)
    line, near, far = lax.optimization_barrier((line, near, far))
    columns = Z * part
    full = (columns, width)

    s, th, tm = [], [], []
    for b, texts in enumerate((line, flip(line, "core", 2, 1))):
        outs = [
            ((2 * rows, columns), F32, rows_at((STEP, columns))),
            (full, BF16, whole(full)),
            (full, BF16, whole(full)),
        ] + table
        if b == 0:
            ins = [pl.BlockSpec(tall, lambda i: (jnp.minimum(i, 1), 0)), whole(tall), whole(tall)]
            outs += [((2 * rows, width), BF16, rows_at(tall))] * 3
            args = (image, near, far)
        else:
            ins = [rows_at(tall)] * 3 + [spec for _, _, spec in table]
            args = (ih, im, il, r, c)
        out = grid_call(
            functools.partial(scores_kernel, b == 0),
            "scores",
            2 * steps,
            [SMEM] + ins + [whole(full)],
            outs,
            scratch=[pltpu.VMEM((width, columns), BF16)] * 3 + [pltpu.VMEM((1, columns), F32)] * 2,
            free_in=(6,) if b else (2, 3),
        )(place, *args, texts)
        s.append(out[0])
        th.append(out[1])
        tm.append(out[2])
        r, c = out[3:5]
        if b == 0:
            ih, im, il = out[5:]

    c = c.reshape(2, Z, part)
    rounds = zip(
        (("y", 4, 1), ("y", 4, 2), ("xl", 2, 1), ("xh", 2, 1)),
        (("core", 2, 1), ("z", 8, 1), ("z", 8, 2), ("z", 8, 4)),
    )
    for row_round, col_round in rounds:
        r, c = join(r, flip(r, *row_round)), join(c, flip(c, *col_round))

    c = c.reshape(2, columns)
    args = (s[0], s[1], r, c, th[0], tm[0], th[1], tm[1])
    sizes = [a.shape[1] for a in s]
    kept = [((rows, n), BF16, rows_at((STEP, n))) for n in sizes for _ in range(2)]
    fixed = [spec for _, _, spec in table] + [whole((n, width)) for n in sizes for _ in range(2)]
    away = grid_call(
        functools.partial(rows_kernel, 1),
        "away",
        steps,
        [SMEM] + [rows_at((STEP, n), steps) for n in sizes] + fixed,
        [((half, width), F32, whole((half, width)))] * 2 + kept,
    )(place, *args)
    got = swap_x(*away[:2])
    kept_away = away[2:]
    late, _ = lax.optimization_barrier((args, away[0]))
    home = grid_call(
        functools.partial(rows_kernel, 0),
        "home",
        steps,
        [SMEM] + [rows_at((STEP, n)) for n in sizes] + fixed,
        [((rows, width), F32, rows_at(tall))] + kept,
        free_out=(0,),
    )(place, *late)
    home, kept_home = home[0], home[1:]

    def make_text(b, name, outs):
        wide = pl.BlockSpec((rows, STEP), lambda i: (0, i))
        return grid_call(
            text_kernel,
            name,
            columns // STEP,
            [wide] * 4 + [whole((2 * rows, width))] * 2,
            outs,
            free_out=(0,) if len(outs) == 1 else (),
        )(*kept_home[2 * b : 2 * b + 2], *kept_away[2 * b : 2 * b + 2], ih, im)

    piece = (columns // CUTS, width)
    other = make_text(1, "text_other", [(piece, F32, whole(piece))] * CUTS)
    (own,) = make_text(0, "text_own", [(full, F32, rows_at(tall))])
    pieces = [flip(a, "core", 2, 1) for a in other]
    (g_text,) = call(collect_kernel, "collect", [(full, F32)], 1 + len(pieces))(own, *pieces)
    g_text, *got = lax.optimization_barrier((g_text, *got))
    grad_text = lax.psum_scatter(g_text, "z", scatter_dimension=0, tiled=True)

    def over_y(pieces):
        return pieces[0] + sum(lax.ppermute(pieces[k], "y", ring(Y, k)) for k in (1, 3, 2))

    def to_y(own):
        return [own] + [lax.ppermute(own, "y", ring(Y, k)) for k in (1, 2, 3)]

    each = width - WIDE
    picked = call(
        pick_kernel, "pick", [((rows // Y, each), F32)] * Y + [((half, WIDE), F32)] * 2, 3, scalars=True, cost=PICK
    )(place, home, *got)
    got, first = lax.optimization_barrier((flip(picked[Y + 1], "xh", 2, 1), over_y(picked[:Y])))
    terms = call(turn_kernel, "turn", [((half // Y, WIDE), F32)] * Y, 2, scalars=True)(place, picked[Y], got)
    second, first = lax.optimization_barrier((over_y(terms), first + flip(first, "xh", 2, 1)))
    second = to_y(second)
    (second,) = call(gather_kernel, "gather", [((half, WIDE), F32)], Y, scalars=True)(place, *second)
    (out,) = call(assemble_kernel, "assemble", [((rows, width), F32)], Y + 2, scalars=True)(
        place, *to_y(first), second, flip(second, "xh", 2, 1)
    )
    return out, grad_text


def solution(mesh):
    fine = Mesh(mesh.devices.reshape(Z, 2, 2, Y, 2), ("z", "xl", "core", "y", "xh"))
    blk = ("z", "xl", "core")
    placed = (P(blk, None), P(blk + ("y", "xh"), None))
    return jax.shard_map(local, mesh=fine, in_specs=placed, out_specs=placed, check_vma=False)
```

```python
import functools

import jax
import jax.numpy as jnp
from jax import lax
from jax.experimental import pallas as pl
from jax.experimental.pallas import tpu as pltpu
from jax.sharding import Mesh, PartitionSpec as P

Z, Y = 8, 4
STEP = 256
CUTS = 8
WIDE = 512
PICK = 100_000_000
F32, BF16 = jnp.float32, jnp.bfloat16
VMEM = pl.BlockSpec(memory_space=pltpu.VMEM)
SMEM = pl.BlockSpec(memory_space=pltpu.SMEM)


def call(kernel, name, outs, n_in, scalars=False, scratch=(), cost=1000):
    in_specs = [VMEM] * n_in
    if scalars:
        in_specs = [SMEM] + in_specs
    return pl.pallas_call(
        kernel,
        out_shape=tuple(jax.ShapeDtypeStruct(s, t) for s, t in outs),
        in_specs=in_specs,
        out_specs=(VMEM,) * len(outs),
        scratch_shapes=scratch,
        compiler_params=pltpu.CompilerParams(vmem_limit_bytes=24 * 1024 * 1024),
        cost_estimate=pl.CostEstimate(flops=1000, bytes_accessed=cost, transcendentals=0),
        name=name,
    )


def grid_call(kernel, name, steps, ins, outs, scratch=(), cost=1000, free_in=(), free_out=()):
    run = pl.pallas_call(
        kernel,
        grid=(steps,),
        out_shape=tuple(
            jax.ShapeDtypeStruct(s, t) if k in free_out else pltpu.HBM(s, t) for k, (s, t, _) in enumerate(outs)
        ),
        in_specs=list(ins),
        out_specs=tuple(spec for _, _, spec in outs),
        scratch_shapes=scratch,
        compiler_params=pltpu.CompilerParams(
            vmem_limit_bytes=40 * 1024 * 1024, dimension_semantics=("arbitrary",)
        ),
        cost_estimate=pl.CostEstimate(flops=1000, bytes_accessed=cost, transcendentals=0),
        name=name,
    )

    def apply(*args):
        return run(
            *[
                a if k == 0 and ins[0] is SMEM or k in free_in else pltpu.with_memory_space_constraint(a, pltpu.HBM)
                for k, a in enumerate(args)
            ]
        )

    return apply


def rows_at(block, start=0):
    return pl.BlockSpec(block, lambda i: (i + start, 0))


def whole(block):
    return pl.BlockSpec(block, lambda i: (0,) * len(block))


def ring(n, step):
    return [(i, (i + step) % n) for i in range(n)]


def flip(a, axis, size, bit):
    return lax.ppermute(a, axis, [(i, i ^ bit) for i in range(size)])


def x_other():
    pairs = []
    for x in range(4):
        t = (x - 1) % 4 if x % 2 == 0 else (x + 1) % 4
        pairs.append(((x % 2) * 2 + x // 2, (t % 2) * 2 + t // 2))
    return pairs


def swap_x(near, far):
    return flip(near, "xl", 2, 1), lax.ppermute(far, ("xl", "xh"), x_other())


def join(a, b):
    top = jnp.maximum(a, b)
    return top + jnp.log(1.0 + jnp.exp(jnp.minimum(a, b) - top))


def split2(a):
    high = a.astype(BF16)
    return high, (a - high.astype(F32)).astype(BF16)


def split3(a):
    high = a.astype(BF16)
    rest = a - high.astype(F32)
    mid = rest.astype(BF16)
    return high, mid, (rest - mid.astype(F32)).astype(BF16)


def dot(a, b, dims=((1,), (0,))):
    return lax.dot_general(a, b, (dims, ((), ())), preferred_element_type=F32)


def split_image_kernel(image_ref, near_ref, far_ref, h_ref, m_ref, l_ref):
    i = pl.program_id(0)
    a = jnp.where(i < 2, image_ref[...], jnp.where(i == 2, near_ref[...], far_ref[...]))
    h_ref[...], m_ref[...], l_ref[...] = split3(a)


def scores_kernel(first, place, *refs):
    i = pl.program_id(0)
    ih_ref, im_ref, il_ref = refs[:3]
    if not first:
        r_in, c_in = refs[3:5]
    text_ref, s_ref, th_ref, tm_ref, r_ref, c_ref = refs[-11:-5]
    h_t, m_t, l_t, top, total = refs[-5:]

    @pl.when(i == 0)
    def _():
        text = text_ref[...]
        th_ref[...], tm_ref[...] = split2(text)
        h_t[...], m_t[...], l_t[...] = split3(text.T)
        top[...] = jnp.full(top.shape, -jnp.inf, F32)
        total[...] = jnp.zeros(total.shape, F32)
        if first:
            c_ref[...] = jnp.zeros(c_ref.shape, F32)
        else:
            c_ref[...] = c_in[...]

    ih, im, il = ih_ref[...], im_ref[...], il_ref[...]
    th, tm, tl = h_t[...], m_t[...], l_t[...]
    small = dot(ih, tl) + dot(il, th) + dot(im, tm)
    s = dot(ih, th) + (dot(ih, tm) + dot(im, th) + small)
    s_ref[...] = s
    high = jnp.max(s, axis=1, keepdims=True)
    row = high + jnp.log(jnp.sum(jnp.exp(s - high), axis=1, keepdims=True))
    row = jnp.broadcast_to(row, (row.shape[0], 128)).T[:1, :]
    slot = pl.ds((i + 2 * place[0]) % 4, 1)
    r_ref[slot, :] = row if first else join(row, r_in[slot, :])
    high = jnp.maximum(jnp.max(s, axis=0, keepdims=True), top[...])
    total[...] = total[...] * jnp.exp(top[...] - high) + jnp.sum(jnp.exp(s - high), axis=0, keepdims=True)
    top[...] = high

    @pl.when(i == pl.num_programs(0) - 1)
    def _():
        core = place[1] if first else 1 - place[1]
        c_ref[pl.ds(core, 1), :] = top[...] + jnp.log(total[...])


def weights(s, row, col):
    return 0.5 * jnp.exp(s - row) + 0.5 * jnp.exp(s - col)


def rows_kernel(away, place, s1, s2, r_ref, c_ref, th1, tm1, th2, tm2, *refs):
    i = pl.program_id(0)
    if away:
        near, far = refs[:2]
    kept = refs[2 if away else 1 :]
    part = c_ref.shape[1] // Z

    c1, c2 = (c_ref[pl.ds(a, 1), :] for a in (place[1], 1 - place[1]))
    row = r_ref[pl.ds((i + 2 * away + 2 * place[0]) % 4, 1), :]
    row = jnp.broadcast_to(row, (128, row.shape[1])).T[:, :1]
    total = None
    for b, (s, c, th, tm) in enumerate(((s1, c1, th1, tm1), (s2, c2, th2, tm2))):
        w = weights(s[...], row, c)
        if b == 0 and not away:
            x = lax.broadcasted_iota(jnp.int32, w.shape, 0) + (i * w.shape[0] - place[3])
            y = lax.broadcasted_iota(jnp.int32, w.shape, 1) - place[2] * part
            w = jnp.where((x == y) & (y >= 0) & (y < part), w - 1.0, w)
        wh, wl = split2(w)
        kept[2 * b][...], kept[2 * b + 1][...] = wh, wl
        term = dot(wh, th[...]) + (dot(wh, tm[...]) + dot(wl, th[...]))
        total = term if total is None else total + term
    if not away:
        refs[0][...] = total
    else:

        @pl.when(i == 0)
        def _():
            near[...] = total

        @pl.when(i == 1)
        def _():
            far[...] = total


def text_kernel(home_h, home_l, away_h, away_l, ih, im, *outs):
    tn = ((0,), (0,))
    rows = home_h.shape[0]
    total = None
    for h, l, k in ((home_h, home_l, 0), (away_h, away_l, rows)):
        high, mid = ih[k : k + rows, :], im[k : k + rows, :]
        wh, wl = h[...], l[...]
        term = dot(wh, high, tn) + (dot(wh, mid, tn) + dot(wl, high, tn))
        total = term if total is None else total + term
    if len(outs) == 1:
        outs[0][...] = total
        return
    n = outs[0].shape[0]
    each = total.shape[0] // n
    for k, out in enumerate(outs):

        @pl.when(pl.program_id(0) == k // each)
        def _():
            out[...] = total[k % each * n : (k % each + 1) * n]


def collect_kernel(own, *refs):
    got, out = refs[:-1], refs[-1]
    n = out.shape[0] // len(got)
    for k, ref in enumerate(got):
        at = slice(k * n, (k + 1) * n)
        out[at, :] = own[at, :] + ref[...]


def pick_kernel(place, home_ref, near_ref, far_ref, *outs):
    size, each = outs[0].shape
    for k in range(Y):
        at = (place[4] + k) % Y
        got = pl.ds((at % 2) * size, size)
        outs[k][...] = home_ref[pl.ds(at * size, size), :each] + jnp.where(
            at < 2, near_ref[got, :each], far_ref[got, :each]
        )
    half = near_ref.shape[0]
    for out, at in ((outs[Y], place[5]), (outs[Y + 1], 1 - place[5])):
        out[...] = home_ref[pl.ds(at * half, half), each:] + jnp.where(at == 0, near_ref[:, each:], far_ref[:, each:])


def turn_kernel(place, kept, got, *outs):
    size = outs[0].shape[0]
    for k in range(Y):
        at = pl.ds((place[4] + k) % Y * size, size)
        outs[k][...] = kept[at, :] + got[at, :]


def gather_kernel(place, *refs):
    pieces, out = refs[:-1], refs[-1]
    size = pieces[0].shape[0]
    for k in range(Y):
        out[pl.ds((place[4] + Y - k) % Y * size, size), :] = pieces[k][...]


def assemble_kernel(place, *refs):
    pieces, halves, out = refs[:Y], refs[Y:-1], refs[-1]
    size, each = pieces[0].shape
    for k in range(Y):
        out[pl.ds((place[4] + Y - k) % Y * size, size), :each] = pieces[k][...]
    size = halves[0].shape[0]
    for half, at in ((halves[0], place[5]), (halves[1], 1 - place[5])):
        out[pl.ds(at * size, size), each:] = half[...]


def local(image, text):
    rows, width = image.shape
    part = text.shape[0]
    z, xl, core, y = (lax.axis_index(a) for a in ("z", "xl", "core", "y"))
    group = y * 2 + lax.axis_index("xh")
    half = rows // 2
    place = jnp.stack([xl, core, z, group * part, y, lax.axis_index("xh")]).astype(jnp.int32)
    tall, steps = (STEP, width), rows // STEP
    table = [((2 * steps, STEP), F32, whole((2 * steps, STEP))), ((2, Z * part), F32, whole((2, Z * part)))]

    near, far = swap_x(image[:half], image[half:])
    line = lax.all_gather(text, "z", axis=0, tiled=True)
    columns = Z * part
    full = (columns, width)
    ih, im, il = grid_call(
        split_image_kernel,
        "split_image",
        2 * steps,
        [pl.BlockSpec(tall, lambda i: (jnp.minimum(i, 1), 0)), whole(tall), whole(tall)],
        [((2 * rows, width), BF16, rows_at(tall))] * 3,
        free_in=(1, 2),
    )(image, near, far)
    line, ih, im, il = lax.optimization_barrier((line, ih, im, il))

    s, th, tm = [], [], []
    for b, texts in enumerate((line, flip(line, "core", 2, 1))):
        carried = () if b == 0 else (r, c)
        a, h, m, r, c = grid_call(
            functools.partial(scores_kernel, b == 0),
            "scores",
            2 * steps,
            [SMEM] + [rows_at(tall)] * 3 + [spec for _, _, spec in table][: len(carried)] + [whole(full)],
            [
                ((2 * rows, columns), F32, rows_at((STEP, columns))),
                (full, BF16, whole(full)),
                (full, BF16, whole(full)),
            ]
            + table,
            scratch=[pltpu.VMEM((width, columns), BF16)] * 3 + [pltpu.VMEM((1, columns), F32)] * 2,
            free_in=(6,) if b else (),
        )(place, ih, im, il, *carried, texts)
        s.append(a)
        th.append(h)
        tm.append(m)

    c = c.reshape(2, Z, part)
    rounds = zip(
        (("y", 4, 1), ("y", 4, 2), ("xl", 2, 1), ("xh", 2, 1)),
        (("core", 2, 1), ("z", 8, 1), ("z", 8, 2), ("z", 8, 4)),
    )
    for row_round, col_round in rounds:
        r, c = join(r, flip(r, *row_round)), join(c, flip(c, *col_round))

    c = c.reshape(2, columns)
    args = (s[0], s[1], r, c, th[0], tm[0], th[1], tm[1])
    sizes = [a.shape[1] for a in s]
    kept = [((rows, n), BF16, rows_at((STEP, n))) for n in sizes for _ in range(2)]
    fixed = [spec for _, _, spec in table] + [whole((n, width)) for n in sizes for _ in range(2)]
    away = grid_call(
        functools.partial(rows_kernel, 1),
        "away",
        steps,
        [SMEM] + [rows_at((STEP, n), steps) for n in sizes] + fixed,
        [((half, width), F32, whole((half, width)))] * 2 + kept,
    )(place, *args)
    got = swap_x(*away[:2])
    kept_away = away[2:]
    late, _ = lax.optimization_barrier((args, away[0]))
    home = grid_call(
        functools.partial(rows_kernel, 0),
        "home",
        steps,
        [SMEM] + [rows_at((STEP, n)) for n in sizes] + fixed,
        [((rows, width), F32, rows_at(tall))] + kept,
        free_out=(0,),
    )(place, *late)
    home, kept_home = home[0], home[1:]

    def make_text(b, name, outs):
        wide = pl.BlockSpec((rows, STEP), lambda i: (0, i))
        return grid_call(
            text_kernel,
            name,
            columns // STEP,
            [wide] * 4 + [whole((2 * rows, width))] * 2,
            outs,
            free_out=(0,) if len(outs) == 1 else (),
        )(*kept_home[2 * b : 2 * b + 2], *kept_away[2 * b : 2 * b + 2], ih, im)

    piece = (columns // CUTS, width)
    other = make_text(1, "text_other", [(piece, F32, whole(piece))] * CUTS)
    (own,) = make_text(0, "text_own", [(full, F32, rows_at(tall))])
    pieces = [flip(a, "core", 2, 1) for a in other]
    (g_text,) = call(collect_kernel, "collect", [(full, F32)], 1 + len(pieces))(own, *pieces)
    g_text, *got = lax.optimization_barrier((g_text, *got))
    grad_text = lax.psum_scatter(g_text, "z", scatter_dimension=0, tiled=True)

    def over_y(pieces):
        return pieces[0] + sum(lax.ppermute(pieces[k], "y", ring(Y, k)) for k in (1, 3, 2))

    def to_y(own):
        return [own] + [lax.ppermute(own, "y", ring(Y, k)) for k in (1, 2, 3)]

    each = width - WIDE
    picked = call(
        pick_kernel, "pick", [((rows // Y, each), F32)] * Y + [((half, WIDE), F32)] * 2, 3, scalars=True, cost=PICK
    )(place, home, *got)
    got, first = lax.optimization_barrier((flip(picked[Y + 1], "xh", 2, 1), over_y(picked[:Y])))
    terms = call(turn_kernel, "turn", [((half // Y, WIDE), F32)] * Y, 2, scalars=True)(place, picked[Y], got)
    second, first = lax.optimization_barrier((over_y(terms), first + flip(first, "xh", 2, 1)))
    second = to_y(second)
    (second,) = call(gather_kernel, "gather", [((half, WIDE), F32)], Y, scalars=True)(place, *second)
    (out,) = call(assemble_kernel, "assemble", [((rows, width), F32)], Y + 2, scalars=True)(
        place, *to_y(first), second, flip(second, "xh", 2, 1)
    )
    return out, grad_text


def solution(mesh):
    fine = Mesh(mesh.devices.reshape(Z, 2, 2, Y, 2), ("z", "xl", "core", "y", "xh"))
    blk = ("z", "xl", "core")
    placed = (P(blk, None), P(blk + ("y", "xh"), None))
    return jax.shard_map(local, mesh=fine, in_specs=placed, out_specs=placed, check_vma=False)
```

```python
import functools

import jax
import jax.numpy as jnp
from jax import lax
from jax.experimental import pallas as pl
from jax.experimental.pallas import tpu as pltpu
from jax.sharding import Mesh, PartitionSpec as P

Z, Y = 8, 4
STEP = 256
CUTS = 8
WIDE = 384
PICK = 100_000_000
F32, BF16 = jnp.float32, jnp.bfloat16
VMEM = pl.BlockSpec(memory_space=pltpu.VMEM)
SMEM = pl.BlockSpec(memory_space=pltpu.SMEM)


def call(kernel, name, outs, n_in, scalars=False, scratch=(), cost=1000):
    in_specs = [VMEM] * n_in
    if scalars:
        in_specs = [SMEM] + in_specs
    return pl.pallas_call(
        kernel,
        out_shape=tuple(jax.ShapeDtypeStruct(s, t) for s, t in outs),
        in_specs=in_specs,
        out_specs=(VMEM,) * len(outs),
        scratch_shapes=scratch,
        compiler_params=pltpu.CompilerParams(vmem_limit_bytes=24 * 1024 * 1024),
        cost_estimate=pl.CostEstimate(flops=1000, bytes_accessed=cost, transcendentals=0),
        name=name,
    )


def grid_call(kernel, name, steps, ins, outs, scratch=(), cost=1000, free_in=(), free_out=()):
    run = pl.pallas_call(
        kernel,
        grid=(steps,),
        out_shape=tuple(
            jax.ShapeDtypeStruct(s, t) if k in free_out else pltpu.HBM(s, t) for k, (s, t, _) in enumerate(outs)
        ),
        in_specs=list(ins),
        out_specs=tuple(spec for _, _, spec in outs),
        scratch_shapes=scratch,
        compiler_params=pltpu.CompilerParams(
            vmem_limit_bytes=40 * 1024 * 1024, dimension_semantics=("arbitrary",)
        ),
        cost_estimate=pl.CostEstimate(flops=1000, bytes_accessed=cost, transcendentals=0),
        name=name,
    )

    def apply(*args):
        return run(
            *[
                a if k == 0 and ins[0] is SMEM or k in free_in else pltpu.with_memory_space_constraint(a, pltpu.HBM)
                for k, a in enumerate(args)
            ]
        )

    return apply


def rows_at(block, start=0):
    return pl.BlockSpec(block, lambda i: (i + start, 0))


def whole(block):
    return pl.BlockSpec(block, lambda i: (0,) * len(block))


def ring(n, step):
    return [(i, (i + step) % n) for i in range(n)]


def flip(a, axis, size, bit):
    return lax.ppermute(a, axis, [(i, i ^ bit) for i in range(size)])


def x_other():
    pairs = []
    for x in range(4):
        t = (x - 1) % 4 if x % 2 == 0 else (x + 1) % 4
        pairs.append(((x % 2) * 2 + x // 2, (t % 2) * 2 + t // 2))
    return pairs


def swap_x(near, far):
    return flip(near, "xl", 2, 1), lax.ppermute(far, ("xl", "xh"), x_other())


def join(a, b):
    top = jnp.maximum(a, b)
    return top + jnp.log(1.0 + jnp.exp(jnp.minimum(a, b) - top))


def split2(a):
    high = a.astype(BF16)
    return high, (a - high.astype(F32)).astype(BF16)


def split3(a):
    high = a.astype(BF16)
    rest = a - high.astype(F32)
    mid = rest.astype(BF16)
    return high, mid, (rest - mid.astype(F32)).astype(BF16)


def dot(a, b, dims=((1,), (0,))):
    return lax.dot_general(a, b, (dims, ((), ())), preferred_element_type=F32)


def split_image_kernel(image_ref, near_ref, far_ref, h_ref, m_ref, l_ref):
    i = pl.program_id(0)
    a = jnp.where(i < 2, image_ref[...], jnp.where(i == 2, near_ref[...], far_ref[...]))
    h_ref[...], m_ref[...], l_ref[...] = split3(a)


def scores_kernel(first, place, *refs):
    i = pl.program_id(0)
    ih_ref, im_ref, il_ref = refs[:3]
    if not first:
        r_in, c_in = refs[3:5]
    text_ref, s_ref, th_ref, tm_ref, r_ref, c_ref = refs[-11:-5]
    h_t, m_t, l_t, top, total = refs[-5:]

    @pl.when(i == 0)
    def _():
        text = text_ref[...]
        th_ref[...], tm_ref[...] = split2(text)
        h_t[...], m_t[...], l_t[...] = split3(text.T)
        top[...] = jnp.full(top.shape, -jnp.inf, F32)
        total[...] = jnp.zeros(total.shape, F32)
        if first:
            c_ref[...] = jnp.zeros(c_ref.shape, F32)
        else:
            c_ref[...] = c_in[...]

    ih, im, il = ih_ref[...], im_ref[...], il_ref[...]
    th, tm, tl = h_t[...], m_t[...], l_t[...]
    small = dot(ih, tl) + dot(il, th) + dot(im, tm)
    s = dot(ih, th) + (dot(ih, tm) + dot(im, th) + small)
    s_ref[...] = s
    high = jnp.max(s, axis=1, keepdims=True)
    row = high + jnp.log(jnp.sum(jnp.exp(s - high), axis=1, keepdims=True))
    row = jnp.broadcast_to(row, (row.shape[0], 128)).T[:1, :]
    slot = pl.ds((i + 2 * place[0]) % 4, 1)
    r_ref[slot, :] = row if first else join(row, r_in[slot, :])
    high = jnp.maximum(jnp.max(s, axis=0, keepdims=True), top[...])
    total[...] = total[...] * jnp.exp(top[...] - high) + jnp.sum(jnp.exp(s - high), axis=0, keepdims=True)
    top[...] = high

    @pl.when(i == pl.num_programs(0) - 1)
    def _():
        core = place[1] if first else 1 - place[1]
        c_ref[pl.ds(core, 1), :] = top[...] + jnp.log(total[...])


def weights(s, row, col):
    return 0.5 * jnp.exp(s - row) + 0.5 * jnp.exp(s - col)


def rows_kernel(away, place, s1, s2, r_ref, c_ref, th1, tm1, th2, tm2, *refs):
    i = pl.program_id(0)
    if away:
        near, far = refs[:2]
    kept = refs[2 if away else 1 :]
    part = c_ref.shape[1] // Z

    c1, c2 = (c_ref[pl.ds(a, 1), :] for a in (place[1], 1 - place[1]))
    row = r_ref[pl.ds((i + 2 * away + 2 * place[0]) % 4, 1), :]
    row = jnp.broadcast_to(row, (128, row.shape[1])).T[:, :1]
    total = None
    for b, (s, c, th, tm) in enumerate(((s1, c1, th1, tm1), (s2, c2, th2, tm2))):
        w = weights(s[...], row, c)
        if b == 0 and not away:
            x = lax.broadcasted_iota(jnp.int32, w.shape, 0) + (i * w.shape[0] - place[3])
            y = lax.broadcasted_iota(jnp.int32, w.shape, 1) - place[2] * part
            w = jnp.where((x == y) & (y >= 0) & (y < part), w - 1.0, w)
        wh, wl = split2(w)
        kept[2 * b][...], kept[2 * b + 1][...] = wh, wl
        term = dot(wh, th[...]) + (dot(wh, tm[...]) + dot(wl, th[...]))
        total = term if total is None else total + term
    if not away:
        refs[0][...] = total
    else:

        @pl.when(i == 0)
        def _():
            near[...] = total

        @pl.when(i == 1)
        def _():
            far[...] = total


def text_kernel(home_h, home_l, away_h, away_l, ih, im, *outs):
    tn = ((0,), (0,))
    rows = home_h.shape[0]
    total = None
    for h, l, k in ((home_h, home_l, 0), (away_h, away_l, rows)):
        high, mid = ih[k : k + rows, :], im[k : k + rows, :]
        wh, wl = h[...], l[...]
        term = dot(wh, high, tn) + (dot(wh, mid, tn) + dot(wl, high, tn))
        total = term if total is None else total + term
    if len(outs) == 1:
        outs[0][...] = total
        return
    n = outs[0].shape[0]
    each = total.shape[0] // n
    for k, out in enumerate(outs):

        @pl.when(pl.program_id(0) == k // each)
        def _():
            out[...] = total[k % each * n : (k % each + 1) * n]


def collect_kernel(own, *refs):
    got, out = refs[:-1], refs[-1]
    n = out.shape[0] // len(got)
    for k, ref in enumerate(got):
        at = slice(k * n, (k + 1) * n)
        out[at, :] = own[at, :] + ref[...]


def pick_kernel(place, home_ref, near_ref, far_ref, *outs):
    size, each = outs[0].shape
    for k in range(Y):
        at = (place[4] + k) % Y
        got = pl.ds((at % 2) * size, size)
        outs[k][...] = home_ref[pl.ds(at * size, size), :each] + jnp.where(
            at < 2, near_ref[got, :each], far_ref[got, :each]
        )
    half = near_ref.shape[0]
    for out, at in ((outs[Y], place[5]), (outs[Y + 1], 1 - place[5])):
        out[...] = home_ref[pl.ds(at * half, half), each:] + jnp.where(at == 0, near_ref[:, each:], far_ref[:, each:])


def turn_kernel(place, kept, got, *outs):
    size = outs[0].shape[0]
    for k in range(Y):
        at = pl.ds((place[4] + k) % Y * size, size)
        outs[k][...] = kept[at, :] + got[at, :]


def gather_kernel(place, *refs):
    pieces, out = refs[:-1], refs[-1]
    size = pieces[0].shape[0]
    for k in range(Y):
        out[pl.ds((place[4] + Y - k) % Y * size, size), :] = pieces[k][...]


def assemble_kernel(place, *refs):
    pieces, halves, out = refs[:Y], refs[Y:-1], refs[-1]
    size, each = pieces[0].shape
    for k in range(Y):
        out[pl.ds((place[4] + Y - k) % Y * size, size), :each] = pieces[k][...]
    size = halves[0].shape[0]
    for half, at in ((halves[0], place[5]), (halves[1], 1 - place[5])):
        out[pl.ds(at * size, size), each:] = half[...]


def local(image, text):
    rows, width = image.shape
    part = text.shape[0]
    z, xl, core, y = (lax.axis_index(a) for a in ("z", "xl", "core", "y"))
    group = y * 2 + lax.axis_index("xh")
    half = rows // 2
    place = jnp.stack([xl, core, z, group * part, y, lax.axis_index("xh")]).astype(jnp.int32)
    tall, steps = (STEP, width), rows // STEP
    table = [((2 * steps, STEP), F32, whole((2 * steps, STEP))), ((2, Z * part), F32, whole((2, Z * part)))]

    near, far = swap_x(image[:half], image[half:])
    line = lax.all_gather(text, "z", axis=0, tiled=True)
    columns = Z * part
    full = (columns, width)
    ih, im, il = grid_call(
        split_image_kernel,
        "split_image",
        2 * steps,
        [pl.BlockSpec(tall, lambda i: (jnp.minimum(i, 1), 0)), whole(tall), whole(tall)],
        [((2 * rows, width), BF16, rows_at(tall))] * 3,
        free_in=(1, 2),
    )(image, near, far)
    line, ih, im, il = lax.optimization_barrier((line, ih, im, il))

    s, th, tm = [], [], []
    for b, texts in enumerate((line, flip(line, "core", 2, 1))):
        carried = () if b == 0 else (r, c)
        a, h, m, r, c = grid_call(
            functools.partial(scores_kernel, b == 0),
            "scores",
            2 * steps,
            [SMEM] + [rows_at(tall)] * 3 + [spec for _, _, spec in table][: len(carried)] + [whole(full)],
            [
                ((2 * rows, columns), F32, rows_at((STEP, columns))),
                (full, BF16, whole(full)),
                (full, BF16, whole(full)),
            ]
            + table,
            scratch=[pltpu.VMEM((width, columns), BF16)] * 3 + [pltpu.VMEM((1, columns), F32)] * 2,
            free_in=(6,) if b else (),
        )(place, ih, im, il, *carried, texts)
        s.append(a)
        th.append(h)
        tm.append(m)

    c = c.reshape(2, Z, part)
    rounds = zip(
        (("y", 4, 1), ("y", 4, 2), ("xl", 2, 1), ("xh", 2, 1)),
        (("core", 2, 1), ("z", 8, 1), ("z", 8, 2), ("z", 8, 4)),
    )
    for row_round, col_round in rounds:
        r, c = join(r, flip(r, *row_round)), join(c, flip(c, *col_round))

    c = c.reshape(2, columns)
    args = (s[0], s[1], r, c, th[0], tm[0], th[1], tm[1])
    sizes = [a.shape[1] for a in s]
    kept = [((rows, n), BF16, rows_at((STEP, n))) for n in sizes for _ in range(2)]
    fixed = [spec for _, _, spec in table] + [whole((n, width)) for n in sizes for _ in range(2)]
    away = grid_call(
        functools.partial(rows_kernel, 1),
        "away",
        steps,
        [SMEM] + [rows_at((STEP, n), steps) for n in sizes] + fixed,
        [((half, width), F32, whole((half, width)))] * 2 + kept,
    )(place, *args)
    got = swap_x(*away[:2])
    kept_away = away[2:]
    late, _ = lax.optimization_barrier((args, away[0]))
    home = grid_call(
        functools.partial(rows_kernel, 0),
        "home",
        steps,
        [SMEM] + [rows_at((STEP, n)) for n in sizes] + fixed,
        [((rows, width), F32, rows_at(tall))] + kept,
        free_out=(0,),
    )(place, *late)
    home, kept_home = home[0], home[1:]

    def make_text(b, name, outs):
        wide = pl.BlockSpec((rows, STEP), lambda i: (0, i))
        return grid_call(
            text_kernel,
            name,
            columns // STEP,
            [wide] * 4 + [whole((2 * rows, width))] * 2,
            outs,
            free_out=(0,) if len(outs) == 1 else (),
        )(*kept_home[2 * b : 2 * b + 2], *kept_away[2 * b : 2 * b + 2], ih, im)

    piece = (columns // CUTS, width)
    other = make_text(1, "text_other", [(piece, F32, whole(piece))] * CUTS)
    (own,) = make_text(0, "text_own", [(full, F32, rows_at(tall))])
    pieces = [flip(a, "core", 2, 1) for a in other]
    (g_text,) = call(collect_kernel, "collect", [(full, F32)], 1 + len(pieces))(own, *pieces)
    g_text, *got = lax.optimization_barrier((g_text, *got))
    grad_text = lax.psum_scatter(g_text, "z", scatter_dimension=0, tiled=True)

    def over_y(pieces):
        return pieces[0] + sum(lax.ppermute(pieces[k], "y", ring(Y, k)) for k in (1, 3, 2))

    def to_y(own):
        return [own] + [lax.ppermute(own, "y", ring(Y, k)) for k in (1, 2, 3)]

    each = width - WIDE
    picked = call(
        pick_kernel, "pick", [((rows // Y, each), F32)] * Y + [((half, WIDE), F32)] * 2, 3, scalars=True, cost=PICK
    )(place, home, *got)
    got, first = lax.optimization_barrier((flip(picked[Y + 1], "xh", 2, 1), over_y(picked[:Y])))
    terms = call(turn_kernel, "turn", [((half // Y, WIDE), F32)] * Y, 2, scalars=True)(place, picked[Y], got)
    second, first = lax.optimization_barrier((over_y(terms), first + flip(first, "xh", 2, 1)))
    second = to_y(second)
    (second,) = call(gather_kernel, "gather", [((half, WIDE), F32)], Y, scalars=True)(place, *second)
    (out,) = call(assemble_kernel, "assemble", [((rows, width), F32)], Y + 2, scalars=True)(
        place, *to_y(first), second, flip(second, "xh", 2, 1)
    )
    return out, grad_text


def solution(mesh):
    fine = Mesh(mesh.devices.reshape(Z, 2, 2, Y, 2), ("z", "xl", "core", "y", "xh"))
    blk = ("z", "xl", "core")
    placed = (P(blk, None), P(blk + ("y", "xh"), None))
    return jax.shard_map(local, mesh=fine, in_specs=placed, out_specs=placed, check_vma=False)
```
